32 devices in a mesh: gx: 4 (over y, core), gy: 8 (over z, x).
Axes of the slice: x: 2, y: 2, z: 4, core: 2. Of those that a mesh axis runs over, the one named last changes fastest.
Arguments:
- displacement: float32 [512, 4096], P('gx', 'gy'), may hold values from -4.2 to 4.2
- velocity: float32 [512, 4096], P('gx', 'gy'), may hold values from -3 to 3
- load: float32 [512, 4096], P('gx', 'gy'), may hold values from -38 to 38
Outputs:
- new_displacement: float32 [512, 4096], P('gx', 'gy')
The draws below stay inside these ranges and needn't reach their ends.
All inputs are finite; a program needn't handle non-finite values.
Results may differ from the reference program's by a relative error of at most 0.000031.
Values sent between devices are 32-bit elements; how exact they have to be, the bound alone decides.
A program may use at most 64 MiB of HBM per device.

```python
import jax
import jax.numpy as jnp

COARSE = 3
NX = 512
NY = 4096


def ramps():
    row_ramp = 1.0 + 0.732 * jnp.arange(NX, dtype=jnp.float32) / NX
    col_ramp = 1.0 + 0.732 * jnp.arange(NY, dtype=jnp.float32) / NY
    return row_ramp[:, None] * col_ramp[None, :]


def rough(key):
    return jnp.clip(jax.random.normal(key, (NX, NY), jnp.float32), -4.0, 4.0)


def draw_displacement(key, part):
    return 0.35 * ramps() * rough(jax.random.fold_in(key, 1))


def draw_velocity(key, part):
    return 0.25 * ramps() * rough(jax.random.fold_in(key, 2))


def draw_load(key, part):
    inner = jax.random.fold_in(key, 3)
    return 8.0 * jnp.clip(jax.random.normal(inner, (NX, NY), jnp.float32), -4.0, 4.0)


def setup_inputs(seed: int = 0) -> dict:
    key_of = jax.random.split(jax.random.key(seed), 4)
    displacement = draw_displacement(jax.random.fold_in(key_of[3], 71), 0)
    velocity = draw_velocity(jax.random.fold_in(key_of[3], 71), 0)
    load = draw_load(jax.random.fold_in(key_of[3], 71), 0)
    return {"displacement": displacement, "velocity": velocity, "load": load}


mass_term = 1e-4
damping = 0.5
tension_base = 1.0
tension_gain = 3.0


def stencil(padded):
    centre = padded[2:-2, 2:-2]
    near_sum = padded[1:-3, 2:-2] + padded[3:-1, 2:-2] + padded[2:-2, 1:-3] + padded[2:-2, 3:-1]
    diag_sum = padded[1:-3, 1:-3] + padded[1:-3, 3:-1] + padded[3:-1, 1:-3] + padded[3:-1, 3:-1]
    far_sum = padded[:-4, 2:-2] + padded[4:, 2:-2] + padded[2:-2, :-4] + padded[2:-2, 4:]
    laplace = 4.0 * centre - near_sum
    biharm = 20.0 * centre - 8.0 * near_sum + 2.0 * diag_sum + far_sum
    return centre, biharm, laplace


def operate(padded, level, tension):
    centre, biharm, laplace = stencil(padded)
    return mass_term * centre + biharm / 16.0 ** level + tension * laplace / 4.0 ** level


def diagonal(level, tension):
    return mass_term + 20.0 / 16.0 ** level + 4.0 * tension / 4.0 ** level


def restrict(field):
    height, breadth = field.shape
    return 0.25 * field.reshape(height // 2, 2, breadth // 2, 2).sum(axis=(1, 3))


def prolong(field):
    return jnp.repeat(jnp.repeat(field, 2, axis=0), 2, axis=1)


def descend(rhs_field, level, tension):
    weight = damping / diagonal(level, tension)
    update = weight * rhs_field
    if level == 3:
        for counter in range(COARSE - 1):
            update = update + weight * (rhs_field - operate(jnp.pad(update, 2), level, tension))
        return update
    leftover = rhs_field - operate(jnp.pad(update, 2), level, tension)
    update = update + prolong(descend(restrict(leftover), level + 1, tension))
    return update + weight * (rhs_field - operate(jnp.pad(update, 2), level, tension))


def reference(displacement, velocity, load):
    predicted = displacement + velocity
    padded = jnp.pad(predicted, 2)
    centre, biharm, laplace = stencil(padded)
    down_diff = padded[3:-1, 2:-2] - predicted
    right_diff = padded[2:-2, 3:-1] - predicted
    energy = jnp.sum(down_diff * down_diff + right_diff * right_diff)
    tension = tension_base + tension_gain * energy / (NX * NY)
    rhs_field = load - (mass_term * centre + biharm + tension * laplace)
    return predicted + descend(rhs_field, 0, tension)
```

```python
import jax
import jax.numpy as jnp
from jax import lax
from jax.experimental import pallas as pl
from jax.experimental.pallas import tpu as pltpu
from jax.sharding import PartitionSpec as P

COARSE = 3
MASS = 0.0001
DAMPING = 0.5
TENSION_BASE = 1.0
TENSION_GAIN = 3.0

HALO = 64
PAD = 8
LANES = 128
CHUNK = 32
MESH = pl.DeviceIdType.MESH


def near(x):
    rows, cols = x.shape
    across = pltpu.roll(x, 1, 1) + pltpu.roll(x, cols - 1, 1)
    return across + (pltpu.roll(x, 1, 0) + pltpu.roll(x, rows - 1, 0))


def constants(level, tension):
    alpha = 1.0 / 16.0**level
    beta = tension * (1.0 / 4.0**level)
    weight = DAMPING / (MASS + 20.0 * alpha + 4.0 * beta)
    return alpha, beta, weight


def operate(x, alpha, beta):
    y = (4.0 * alpha + beta) * x - alpha * near(x)
    return MASS * x + (4.0 * y - near(y))


def dot2(x, matrix):
    high = x.astype(jnp.bfloat16)
    low = (x - high.astype(jnp.float32)).astype(jnp.bfloat16)
    return jnp.dot(high, matrix, preferred_element_type=jnp.float32) + jnp.dot(
        low, matrix, preferred_element_type=jnp.float32
    )


def halo_parent(lane, width):
    right = lane < width
    left = lane >= LANES - width
    upper = LANES - width // 2 + ((lane - (LANES - width)) >> 1)
    return jnp.where(right, lane >> 1, jnp.where(left, upper, -1))


def last_parent(lane, centre, width):
    halo = lane - centre
    right = centre // 2 + (halo >> 1)
    left = LANES - width // 2 + ((halo - (LANES - width)) >> 1)
    outer = jnp.where(halo < width, right, jnp.where(halo >= LANES - width, left, -1))
    return jnp.where(lane < centre, lane >> 1, outer)


def build(ref, parent, value, transposed):
    fine_dim = 1 if transposed else 0
    fine = lax.broadcasted_iota(jnp.int32, ref.shape, fine_dim)
    coarse = lax.broadcasted_iota(jnp.int32, ref.shape, 1 - fine_dim)
    ref[...] = jnp.where(parent(fine) == coarse, value, 0.0).astype(jnp.bfloat16)


def kernel_body(
    nx, ny, height, breadth,
    d_hbm, v_hbm, load_hbm, out_ref,
    dbuf, vbuf, pbuf, lbuf, lmsg, rmsg, from_right, from_left, edge, abuf, bbuf,
    rtile, etile0, r1t, e1t, r2t, e2t,
    mask1, mask2, mask3,
    c2, ch0, ch1, c3, p2, ph0, ph1, p3,
    part, part2, sums_x, sums_y,
    in_sem, send_sem, recv_sem, red_sem,
):
    gx = lax.axis_index("gx")
    gy = lax.axis_index("gy")
    has_up = gx > 0
    has_down = gx < nx - 1
    has_left = gy > 0
    has_right = gy < ny - 1
    total_rows = height + 2 * HALO
    tiles = breadth // LANES
    width = breadth + LANES

    barrier = pltpu.get_barrier_semaphore()
    for step in range(1, nx):
        pl.semaphore_signal(barrier, 1, device_id=(lax.rem(gx + step, nx), gy), device_id_type=MESH)
    for step in range(1, ny):
        pl.semaphore_signal(barrier, 1, device_id=(gx, lax.rem(gy + step, ny)), device_id_type=MESH)
    diagonals = []
    for dx, okx in ((-1, has_up), (1, has_down)):
        for dy, oky in ((-1, has_left), (1, has_right)):
            ok = jnp.logical_and(okx, oky)
            diagonals.append((dx, dy, ok))

            @pl.when(ok)
            def _(dx=dx, dy=dy):
                pl.semaphore_signal(barrier, 1, device_id=(gx + dx, gy + dy), device_id_type=MESH)

    centre_rows = pl.ds(PAD + HALO, height)
    loads = [
        pltpu.make_async_copy(d_hbm, dbuf, in_sem.at[0]),
        pltpu.make_async_copy(v_hbm, vbuf, in_sem.at[1]),
        pltpu.make_async_copy(load_hbm, lbuf.at[centre_rows, pl.ds(0, breadth)], in_sem.at[2]),
    ]
    for copy in loads:
        copy.start()

    zero_rows = jnp.zeros((PAD, width), jnp.float32)
    for buf in (pbuf, lbuf, abuf, bbuf):
        buf[pl.ds(0, PAD), :] = zero_rows
        buf[pl.ds(PAD + total_rows, PAD), :] = zero_rows

    def clear(ref, start, rows, cols):
        ref[pl.ds(start, rows), pl.ds(0, cols)] = jnp.zeros((rows, cols), jnp.float32)

    @pl.when(jnp.logical_not(has_up))
    def _():
        for buf in (pbuf, lbuf):
            clear(buf, PAD, HALO, breadth)
        clear(from_right, 0, HALO, LANES)
        clear(from_left, 0, HALO, LANES)

    @pl.when(jnp.logical_not(has_down))
    def _():
        for buf in (pbuf, lbuf):
            clear(buf, PAD + HALO + height, HALO, breadth)
        clear(from_right, HALO + height, HALO, LANES)
        clear(from_left, HALO + height, HALO, LANES)
        clear(edge, 0, 8, breadth)

    @pl.when(jnp.logical_not(has_right))
    def _():
        clear(from_right, 0, total_rows, LANES)

    @pl.when(jnp.logical_not(has_left))
    def _():
        clear(from_left, 0, total_rows, LANES)

    loads[0].wait()
    loads[1].wait()
    pbuf[centre_rows, pl.ds(0, breadth)] = dbuf[...] + vbuf[...]
    loads[2].wait()

    lane = lax.broadcasted_iota(jnp.int32, (height, LANES), 1)
    first = lane < HALO
    lmsg[...] = jnp.where(
        first,
        pbuf[centre_rows, pl.ds(0, LANES)],
        pltpu.roll(lbuf[centre_rows, pl.ds(0, LANES)], HALO, 1),
    )
    end = pl.ds(breadth - LANES, LANES)
    rmsg[...] = jnp.where(
        first, pltpu.roll(lbuf[centre_rows, end], HALO, 1), pbuf[centre_rows, end]
    )

    wide = pl.ds(0, breadth)
    top_src = pl.ds(PAD + HALO, HALO)
    bottom_src = pl.ds(PAD + height, HALO)
    top_dst = pl.ds(PAD, HALO)
    bottom_dst = pl.ds(PAD + HALO + height, HALO)
    mid = pl.ds(HALO, height)
    upper, lower = pl.ds(0, HALO), pl.ds(height - HALO, HALO)
    dst_top, dst_bottom = pl.ds(0, HALO), pl.ds(HALO + height, HALO)
    both = jnp.logical_and
    plan = [
        (pbuf.at[pl.ds(PAD + HALO, 8), wide], edge, -1, 0, has_up, has_down),
        (lmsg, from_right.at[mid], 0, -1, has_left, has_right),
        (pbuf.at[top_src, wide], pbuf.at[bottom_dst, wide], -1, 0, has_up, has_down),
        (pbuf.at[bottom_src, wide], pbuf.at[top_dst, wide], 1, 0, has_down, has_up),
        (rmsg, from_left.at[mid], 0, 1, has_right, has_left),
        (lmsg.at[upper], from_right.at[dst_bottom], -1, -1, both(has_up, has_left), both(has_down, has_right)),
        (lmsg.at[lower], from_right.at[dst_top], 1, -1, both(has_down, has_left), both(has_up, has_right)),
        (rmsg.at[upper], from_left.at[dst_bottom], -1, 1, both(has_up, has_right), both(has_down, has_left)),
        (rmsg.at[lower], from_left.at[dst_top], 1, 1, both(has_down, has_right), both(has_up, has_left)),
        (lbuf.at[top_src, wide], lbuf.at[bottom_dst, wide], -1, 0, has_up, has_down),
        (lbuf.at[bottom_src, wide], lbuf.at[top_dst, wide], 1, 0, has_down, has_up),
    ]

    def copy_of(index):
        source, target, dx, dy, _, _ = plan[index]
        return pltpu.make_async_remote_copy(
            src_ref=source,
            dst_ref=target,
            send_sem=send_sem.at[index],
            recv_sem=recv_sem.at[index],
            device_id=(gx + dx, gy + dy),
            device_id_type=MESH,
        )

    def received(index):
        @pl.when(plan[index][5])
        def _():
            copy_of(index).wait_recv()

    count = nx - 1 + ny - 1
    for _, _, ok in diagonals:
        count = count + ok.astype(jnp.int32)
    pl.semaphore_wait(barrier, count)
    for index in range(len(plan)):
        @pl.when(plan[index][4])
        def _(index=index):
            copy_of(index).start()

    x = pbuf[centre_rows, wide]
    row = lax.broadcasted_iota(jnp.int32, (height, breadth), 0)
    col = lax.broadcasted_iota(jnp.int32, (height, breadth), 1)
    down = jnp.where(row < height - 1, pltpu.roll(x, height - 1, 0) - x, 0.0)
    right = jnp.where(col < breadth - 1, pltpu.roll(x, breadth - 1, 1) - x, 0.0)
    inner = jnp.sum(down * down + right * right, axis=0, keepdims=True)
    inner = sum(inner[:, t * LANES : (t + 1) * LANES] for t in range(tiles))

    received(0)
    received(1)
    below = edge[pl.ds(0, 1), :] - x[height - 1 : height, :]
    below = below * below
    below = sum(below[:, t * LANES : (t + 1) * LANES] for t in range(tiles))
    beside = from_right[mid, :] - pltpu.roll(x[:, breadth - LANES :], 1, 1)
    beside = jnp.where(lane == 0, beside * beside, 0.0)
    part[...] = inner + below + jnp.sum(beside, axis=0, keepdims=True)

    def reduce_copy(source, slots, step, axis):
        slot = step - 1
        target = (lax.rem(gx + step, nx), gy) if axis == 0 else (gx, lax.rem(gy + step, ny))
        return pltpu.make_async_remote_copy(
            src_ref=source,
            dst_ref=slots.at[slot],
            send_sem=red_sem.at[axis, 0, slot],
            recv_sem=red_sem.at[axis, 1, slot],
            device_id=target,
            device_id_type=MESH,
        )

    along_x = [reduce_copy(part, sums_x, step, 0) for step in range(1, nx)]
    for copy in along_x:
        copy.start()

    build(c2, lambda i: i >> 1, 0.25, False)
    build(p2, lambda i: i >> 1, 1.0, True)
    build(ch0, lambda i: halo_parent(i, HALO), 0.25, False)
    build(ph0, lambda i: halo_parent(i, HALO), 1.0, True)
    build(ch1, lambda i: halo_parent(i, HALO // 2), 0.25, False)
    build(ph1, lambda i: halo_parent(i, HALO // 2), 1.0, True)
    build(c3, lambda i: last_parent(i, LANES, HALO // 4), 0.25, False)
    build(p3, lambda i: last_parent(i, LANES, HALO // 4), 1.0, True)
    up_f, down_f = has_up.astype(jnp.float32), has_down.astype(jnp.float32)
    left_f, right_f = has_left.astype(jnp.float32), has_right.astype(jnp.float32)

    def lane_mask(cols, centre):
        i = lax.broadcasted_iota(jnp.int32, (1, cols), 1)
        outside = jnp.where(i - centre < (cols - centre) // 2, right_f, left_f)
        return jnp.where(i < centre, 1.0, outside)

    for level, mask in ((1, mask1), (2, mask2), (3, mask3)):
        rim, core = HALO >> level, height >> level
        cols = lane_mask(mask.shape[1], breadth >> level)
        mask[pl.ds(0, rim), :] = jnp.broadcast_to(cols * up_f, (rim, mask.shape[1]))
        mask[pl.ds(rim, core), :] = jnp.broadcast_to(cols, (core, mask.shape[1]))
        mask[pl.ds(rim + core, rim), :] = jnp.broadcast_to(cols * down_f, (rim, mask.shape[1]))

    for copy in along_x:
        copy.wait_recv()
    part2[...] = part[...] + sum(sums_x[i] for i in range(nx - 1))
    along_y = [reduce_copy(part2, sums_y, step, 1) for step in range(1, ny)]
    for copy in along_y:
        copy.start()

    for index in range(2, len(plan)):
        received(index)
    halo_first = lax.broadcasted_iota(jnp.int32, (total_rows, LANES), 1) < HALO
    body_rows = pl.ds(PAD, total_rows)
    outer = pl.ds(breadth, LANES)
    fr, fl = from_right[...], from_left[...]
    pbuf[body_rows, outer] = jnp.where(halo_first, fr, fl)
    lbuf[body_rows, outer] = pltpu.roll(jnp.where(halo_first, fl, fr), HALO, 1)
    fine_mask = lane_mask(width, breadth)

    def prepare(chunk, carry):
        start = pl.multiple_of(chunk * CHUNK, CHUNK)
        x = pbuf[pl.ds(start, CHUNK + 2 * PAD), :]
        s = 4.0 * x - near(x)
        q = 4.0 * s - near(s)
        inside = slice(PAD, PAD + CHUNK)
        rows = pl.ds(pl.multiple_of(start + PAD, 8), CHUNK)
        scale = jnp.where(
            start < HALO, up_f, jnp.where(start >= HALO + height, down_f, 1.0)
        )
        mask = fine_mask * scale
        abuf[rows, :] = (lbuf[rows, :] - MASS * x[inside] - q[inside]) * mask
        bbuf[rows, :] = s[inside] * mask
        return carry

    lax.fori_loop(0, total_rows // CHUNK, prepare, 0)

    for copy in along_y:
        copy.wait_recv()
    energy = jnp.sum(part2[...] + sum(sums_y[i] for i in range(ny - 1)))
    cells = float(height * nx * breadth * ny)
    tension = TENSION_BASE + TENSION_GAIN * energy * (1.0 / cells)

    alpha0, beta0, w0 = constants(0, tension)

    def leave(chunk, carry):
        start = pl.multiple_of(chunk * CHUNK, CHUNK)
        rows = pl.ds(start, CHUNK + 2 * PAD)
        g = abuf[rows, :] - tension * bbuf[rows, :]
        r = (g - w0 * operate(g, alpha0, beta0))[PAD : PAD + CHUNK]
        for t in range(tiles + 1):
            at = pl.multiple_of(t * total_rows + start, 8)
            rtile[pl.ds(at, CHUNK), :] = r[:, t * LANES : (t + 1) * LANES]
        return carry

    lax.fori_loop(0, total_rows // CHUNK, leave, 0)

    def paired(ref, rows, count):
        return [
            ref[pl.ds(t * rows, rows // 2, stride=2), :]
            + ref[pl.ds(t * rows + 1, rows // 2, stride=2), :]
            for t in range(count)
        ]

    def restrict(ref, rows, count, halo_matrix):
        xs = paired(ref, rows, count)
        outs = [
            dot2(jnp.concatenate(xs[t : t + 2], axis=1), c2[...])
            for t in range(0, count - 1, 2)
        ]
        outs.append(dot2(xs[-1], halo_matrix[...]))
        return jnp.concatenate(outs, axis=1)

    def spread(ref, columns, rows):
        for t, x in enumerate(columns):
            ref[pl.ds(t * rows, rows // 2, stride=2), :] = x
            ref[pl.ds(t * rows + 1, rows // 2, stride=2), :] = x

    def prolong(ref, e, rows, halo_matrix):
        count = e.shape[1] // LANES
        columns = []
        for t in range(count - 1):
            pair = dot2(e[:, t * LANES : (t + 1) * LANES], p2[...])
            columns += [pair[:, :LANES], pair[:, LANES:]]
        columns.append(dot2(e[:, (count - 1) * LANES :], halo_matrix[...]))
        spread(ref, columns, rows)

    def gathered(ref, rows, count, first_row, n):
        return jnp.concatenate(
            [ref[pl.ds(t * rows + first_row, n), :] for t in range(count)], axis=1
        )

    def store_tiles(ref, value, rows):
        for t in range(value.shape[1] // LANES):
            ref[pl.ds(t * rows, rows), :] = value[:, t * LANES : (t + 1) * LANES]

    rows1, rows2, rows3 = total_rows // 2, total_rows // 4, total_rows // 8
    count1, count2 = tiles // 2 + 1, tiles // 4 + 1

    g1 = restrict(rtile, total_rows, tiles + 1, ch0) * mask1[...]
    alpha1, beta1, w1 = constants(1, tension)
    store_tiles(r1t, g1 - w1 * operate(g1, alpha1, beta1), rows1)
    g2 = restrict(r1t, rows1, count1, ch1) * mask2[...]
    alpha2, beta2, w2 = constants(2, tension)
    store_tiles(r2t, g2 - w2 * operate(g2, alpha2, beta2), rows2)
    pair = paired(r2t, rows2, count2)
    g3 = dot2(jnp.concatenate(pair, axis=1), c3[...]) * mask3[...]

    alpha3, beta3, w3 = constants(3, tension)
    u3 = w3 * g3
    for _ in range(COARSE - 1):
        u3 = (u3 + w3 * (g3 - operate(u3, alpha3, beta3))) * mask3[...]

    wide_pair = dot2(u3, p3[...])
    spread(e2t, [wide_pair[:, :LANES], wide_pair[:, LANES:]], rows2)
    u2 = w2 * g2 + gathered(e2t, rows2, count2, 0, rows2)
    u2 = (u2 + w2 * (g2 - operate(u2, alpha2, beta2))) * mask2[...]
    prolong(e1t, u2, rows1, ph1)
    u1 = w1 * g1 + gathered(e1t, rows1, count1, 0, rows1)
    u1 = (u1 + w1 * (g1 - operate(u1, alpha1, beta1))) * mask1[...]
    prolong(etile0, u1, total_rows, ph0)

    def finish(chunk, carry):
        start = pl.multiple_of(chunk * CHUNK, CHUNK)
        rows = pl.ds(pl.multiple_of(start + HALO, 8), CHUNK + 2 * PAD)
        g = abuf[rows, :] - tension * bbuf[rows, :]
        e = jnp.concatenate(
            [
                etile0[pl.ds(pl.multiple_of(t * total_rows + start + HALO - PAD, 8), CHUNK + 2 * PAD), :]
                for t in range(tiles + 1)
            ],
            axis=1,
        )
        u = w0 * g + e
        u = (u + w0 * (g - operate(u, alpha0, beta0)))[PAD : PAD + CHUNK, :breadth]
        here = pl.ds(pl.multiple_of(start + HALO + PAD, 8), CHUNK)
        out_ref[pl.ds(start, CHUNK), :] = pbuf[here, wide] + u
        return carry

    lax.fori_loop(0, height // CHUNK, finish, 0)

    for copy in along_x + along_y:
        copy.wait_send()
    for index in range(len(plan)):
        @pl.when(plan[index][4])
        def _(index=index):
            copy_of(index).wait_send()


def body(displacement, velocity, load):
    nx, ny = lax.axis_size("gx"), lax.axis_size("gy")
    height, breadth = displacement.shape
    rows, tiles = height + 2 * HALO, breadth // LANES
    padded = (rows + 2 * PAD, breadth + LANES)
    f32, bf16 = jnp.float32, jnp.bfloat16
    widths = [(breadth >> level) + LANES for level in range(3)] + [LANES]

    def vmem(*shape, dtype=f32):
        return pltpu.VMEM(shape, dtype)

    def tiled(level):
        return vmem(widths[level] // LANES * (rows >> level), LANES)

    scratch = [
        vmem(height, breadth), vmem(height, breadth),
        vmem(*padded), vmem(*padded),
        vmem(height, LANES), vmem(height, LANES),
        vmem(rows, LANES), vmem(rows, LANES),
        vmem(8, breadth), vmem(*padded), vmem(*padded),
        tiled(0), tiled(0), tiled(1), tiled(1), tiled(2), tiled(2),
        vmem(rows // 2, widths[1]), vmem(rows // 4, widths[2]), vmem(rows // 8, widths[3]),
        vmem(2 * LANES, LANES, dtype=bf16), vmem(LANES, LANES, dtype=bf16),
        vmem(LANES, LANES, dtype=bf16), vmem(2 * LANES, LANES, dtype=bf16),
        vmem(LANES, 2 * LANES, dtype=bf16), vmem(LANES, LANES, dtype=bf16),
        vmem(LANES, LANES, dtype=bf16), vmem(LANES, 2 * LANES, dtype=bf16),
        vmem(1, LANES), vmem(1, LANES),
        vmem(nx - 1, 1, LANES), vmem(ny - 1, 1, LANES),
        pltpu.SemaphoreType.DMA((3,)),
        pltpu.SemaphoreType.DMA((11,)),
        pltpu.SemaphoreType.DMA((11,)),
        pltpu.SemaphoreType.DMA((2, 2, max(nx, ny) - 1)),
    ]

    def kernel(*refs):
        kernel_body(nx, ny, height, breadth, *refs)

    return pl.pallas_call(
        kernel,
        out_shape=jax.ShapeDtypeStruct((height, breadth), f32),
        in_specs=[pl.BlockSpec(memory_space=pl.ANY)] * 3,
        out_specs=pl.BlockSpec(memory_space=pltpu.VMEM),
        scratch_shapes=scratch,
        compiler_params=pltpu.CompilerParams(
            collective_id=0, has_side_effects=True, vmem_limit_bytes=32 * 1024 * 1024
        ),
    )(displacement, velocity, load)


def solution(mesh):
    placed = (P("gx", "gy"), P("gx", "gy"), P("gx", "gy"))
    return jax.shard_map(body, mesh=mesh, in_specs=placed, out_specs=P("gx", "gy"), check_vma=False)
```

```python
import jax
import jax.numpy as jnp
from jax import lax
from jax.experimental import pallas as pl
from jax.experimental.pallas import tpu as pltpu
from jax.sharding import PartitionSpec as P

COARSE = 3
MASS = 0.0001
DAMPING = 0.5
TENSION_BASE = 1.0
TENSION_GAIN = 3.0

HALO = 64
PAD = 8
LANES = 128
CHUNK = 32
MESH = pl.DeviceIdType.MESH


def near(x):
    rows, cols = x.shape
    across = pltpu.roll(x, 1, 1) + pltpu.roll(x, cols - 1, 1)
    return across + (pltpu.roll(x, 1, 0) + pltpu.roll(x, rows - 1, 0))


def constants(level, tension):
    alpha = 1.0 / 16.0**level
    beta = tension * (1.0 / 4.0**level)
    weight = DAMPING / (MASS + 20.0 * alpha + 4.0 * beta)
    return alpha, beta, weight


def operate(x, alpha, beta):
    y = (4.0 * alpha + beta) * x - alpha * near(x)
    return MASS * x + (4.0 * y - near(y))


def dot2(x, matrix):
    high = x.astype(jnp.bfloat16)
    low = (x - high.astype(jnp.float32)).astype(jnp.bfloat16)
    return jnp.dot(high, matrix, preferred_element_type=jnp.float32) + jnp.dot(
        low, matrix, preferred_element_type=jnp.float32
    )


def halo_parent(lane, width):
    right = lane < width
    left = lane >= LANES - width
    upper = LANES - width // 2 + ((lane - (LANES - width)) >> 1)
    return jnp.where(right, lane >> 1, jnp.where(left, upper, -1))


def last_parent(lane, centre, width):
    halo = lane - centre
    right = centre // 2 + (halo >> 1)
    left = LANES - width // 2 + ((halo - (LANES - width)) >> 1)
    outer = jnp.where(halo < width, right, jnp.where(halo >= LANES - width, left, -1))
    return jnp.where(lane < centre, lane >> 1, outer)


def build(ref, parent, value, transposed):
    fine_dim = 1 if transposed else 0
    fine = lax.broadcasted_iota(jnp.int32, ref.shape, fine_dim)
    coarse = lax.broadcasted_iota(jnp.int32, ref.shape, 1 - fine_dim)
    ref[...] = jnp.where(parent(fine) == coarse, value, 0.0).astype(jnp.bfloat16)


def kernel_body(
    nx, ny, height, breadth,
    d_hbm, v_hbm, load_hbm, out_ref,
    dbuf, vbuf, pbuf, lbuf, lmsg, rmsg, from_right, from_left, edge, rim, rim_in, abuf, bbuf,
    rtile, etile0, r1t, e1t, r2t, e2t,
    mask1, mask2, mask3,
    c2, ch0, ch1, c3, p2, ph0, ph1, p3,
    part, sums,
    in_sem, send_sem, recv_sem, red_sem,
):
    gx = lax.axis_index("gx")
    gy = lax.axis_index("gy")
    has_up = gx > 0
    has_down = gx < nx - 1
    has_left = gy > 0
    has_right = gy < ny - 1
    total_rows = height + 2 * HALO
    tiles = breadth // LANES
    width = breadth + LANES

    barrier = pltpu.get_barrier_semaphore()
    def every_other(action):
        for dx in range(nx):
            ahead = gx + dx
            tx = jnp.where(ahead >= nx, ahead - nx, ahead)

            def at(dy, carry, dx=dx, tx=tx):
                along = gy + dy
                action(dx * ny + dy - 1, (tx, jnp.where(along >= ny, along - ny, along)))
                return carry

            lax.fori_loop(1 if dx == 0 else 0, ny, at, 0, unroll=ny <= 8)

    def greet(slot, device):
        pl.semaphore_signal(barrier, 1, device_id=device, device_id_type=MESH)

    every_other(greet)

    centre_rows = pl.ds(PAD + HALO, height)
    loads = [
        pltpu.make_async_copy(d_hbm, dbuf, in_sem.at[0]),
        pltpu.make_async_copy(v_hbm, vbuf, in_sem.at[1]),
        pltpu.make_async_copy(load_hbm, lbuf.at[centre_rows, pl.ds(0, breadth)], in_sem.at[2]),
    ]
    for copy in loads:
        copy.start()

    zero_rows = jnp.zeros((PAD, width), jnp.float32)
    for buf in (pbuf, lbuf, abuf, bbuf):
        buf[pl.ds(0, PAD), :] = zero_rows
        buf[pl.ds(PAD + total_rows, PAD), :] = zero_rows

    def clear(ref, start, rows, cols):
        ref[pl.ds(start, rows), pl.ds(0, cols)] = jnp.zeros((rows, cols), jnp.float32)

    @pl.when(jnp.logical_not(has_up))
    def _():
        for buf in (pbuf, lbuf):
            clear(buf, PAD, HALO, breadth)
        clear(from_right, 0, HALO, LANES)
        clear(from_left, 0, HALO, LANES)

    @pl.when(jnp.logical_not(has_down))
    def _():
        for buf in (pbuf, lbuf):
            clear(buf, PAD + HALO + height, HALO, breadth)
        clear(from_right, HALO + height, HALO, LANES)
        clear(from_left, HALO + height, HALO, LANES)
        clear(edge, 0, 8, breadth)

    @pl.when(jnp.logical_not(has_right))
    def _():
        clear(from_right, 0, total_rows, LANES)
        clear(rim_in, 0, 8, height)

    @pl.when(jnp.logical_not(has_left))
    def _():
        clear(from_left, 0, total_rows, LANES)

    loads[0].wait()
    loads[1].wait()
    pbuf[centre_rows, pl.ds(0, breadth)] = dbuf[...] + vbuf[...]
    rim[...] = jnp.transpose(pbuf[centre_rows, pl.ds(0, LANES)])[:8]
    loads[2].wait()

    lane = lax.broadcasted_iota(jnp.int32, (height, LANES), 1)
    first = lane < HALO
    lmsg[...] = jnp.where(
        first,
        pbuf[centre_rows, pl.ds(0, LANES)],
        pltpu.roll(lbuf[centre_rows, pl.ds(0, LANES)], HALO, 1),
    )
    end = pl.ds(breadth - LANES, LANES)
    rmsg[...] = jnp.where(
        first, pltpu.roll(lbuf[centre_rows, end], HALO, 1), pbuf[centre_rows, end]
    )

    wide = pl.ds(0, breadth)
    top_src = pl.ds(PAD + HALO, HALO)
    bottom_src = pl.ds(PAD + height, HALO)
    top_dst = pl.ds(PAD, HALO)
    bottom_dst = pl.ds(PAD + HALO + height, HALO)
    mid = pl.ds(HALO, height)
    upper, lower = pl.ds(0, HALO), pl.ds(height - HALO, HALO)
    dst_top, dst_bottom = pl.ds(0, HALO), pl.ds(HALO + height, HALO)
    both = jnp.logical_and
    plan = [
        (pbuf.at[pl.ds(PAD + HALO, 8), wide], edge, -1, 0, has_up, has_down),
        (rim, rim_in, 0, -1, has_left, has_right),
        (pbuf.at[top_src, wide], pbuf.at[bottom_dst, wide], -1, 0, has_up, has_down),
        (pbuf.at[bottom_src, wide], pbuf.at[top_dst, wide], 1, 0, has_down, has_up),
        (lmsg, from_right.at[mid], 0, -1, has_left, has_right),
        (rmsg, from_left.at[mid], 0, 1, has_right, has_left),
        (lmsg.at[upper], from_right.at[dst_bottom], -1, -1, both(has_up, has_left), both(has_down, has_right)),
        (lmsg.at[lower], from_right.at[dst_top], 1, -1, both(has_down, has_left), both(has_up, has_right)),
        (rmsg.at[upper], from_left.at[dst_bottom], -1, 1, both(has_up, has_right), both(has_down, has_left)),
        (rmsg.at[lower], from_left.at[dst_top], 1, 1, both(has_down, has_right), both(has_up, has_left)),
        (lbuf.at[top_src, wide], lbuf.at[bottom_dst, wide], -1, 0, has_up, has_down),
        (lbuf.at[bottom_src, wide], lbuf.at[top_dst, wide], 1, 0, has_down, has_up),
    ]

    def copy_of(index):
        source, target, dx, dy, _, _ = plan[index]
        return pltpu.make_async_remote_copy(
            src_ref=source,
            dst_ref=target,
            send_sem=send_sem.at[index],
            recv_sem=recv_sem.at[index],
            device_id=(gx + dx, gy + dy),
            device_id_type=MESH,
        )

    def received(index):
        @pl.when(plan[index][5])
        def _():
            copy_of(index).wait_recv()

    pl.semaphore_wait(barrier, nx * ny - 1)
    for index in range(len(plan)):
        @pl.when(plan[index][4])
        def _(index=index):
            copy_of(index).start()

    x = pbuf[centre_rows, wide]
    row = lax.broadcasted_iota(jnp.int32, (height, breadth), 0)
    col = lax.broadcasted_iota(jnp.int32, (height, breadth), 1)
    down = jnp.where(row < height - 1, pltpu.roll(x, height - 1, 0) - x, 0.0)
    right = jnp.where(col < breadth - 1, pltpu.roll(x, breadth - 1, 1) - x, 0.0)
    inner = jnp.sum(down * down + right * right, axis=0, keepdims=True)
    inner = sum(inner[:, t * LANES : (t + 1) * LANES] for t in range(tiles))

    last_column = jnp.transpose(x[:, breadth - LANES :])[LANES - 1 :]

    received(0)
    received(1)
    below = edge[pl.ds(0, 1), :] - x[height - 1 : height, :]
    below = below * below
    below = sum(below[:, t * LANES : (t + 1) * LANES] for t in range(tiles))
    beside = rim_in[pl.ds(0, 1), :] - last_column
    beside = beside * beside
    beside = sum(beside[:, t * LANES : (t + 1) * LANES] for t in range(height // LANES))
    part[...] = inner + below + beside

    def give(slot, device):
        pltpu.make_async_remote_copy(
            src_ref=part,
            dst_ref=sums.at[slot],
            send_sem=red_sem.at[0],
            recv_sem=red_sem.at[1],
            device_id=device,
            device_id_type=MESH,
        ).start()

    every_other(give)

    build(c2, lambda i: i >> 1, 0.25, False)
    build(p2, lambda i: i >> 1, 1.0, True)
    build(ch0, lambda i: halo_parent(i, HALO), 0.25, False)
    build(ph0, lambda i: halo_parent(i, HALO), 1.0, True)
    build(ch1, lambda i: halo_parent(i, HALO // 2), 0.25, False)
    build(ph1, lambda i: halo_parent(i, HALO // 2), 1.0, True)
    build(c3, lambda i: last_parent(i, LANES, HALO // 4), 0.25, False)
    build(p3, lambda i: last_parent(i, LANES, HALO // 4), 1.0, True)
    up_f, down_f = has_up.astype(jnp.float32), has_down.astype(jnp.float32)
    left_f, right_f = has_left.astype(jnp.float32), has_right.astype(jnp.float32)

    def lane_mask(cols, centre):
        i = lax.broadcasted_iota(jnp.int32, (1, cols), 1)
        outside = jnp.where(i - centre < (cols - centre) // 2, right_f, left_f)
        return jnp.where(i < centre, 1.0, outside)

    for level, mask in ((1, mask1), (2, mask2), (3, mask3)):
        rim, core = HALO >> level, height >> level
        cols = lane_mask(mask.shape[1], breadth >> level)
        mask[pl.ds(0, rim), :] = jnp.broadcast_to(cols * up_f, (rim, mask.shape[1]))
        mask[pl.ds(rim, core), :] = jnp.broadcast_to(cols, (core, mask.shape[1]))
        mask[pl.ds(rim + core, rim), :] = jnp.broadcast_to(cols * down_f, (rim, mask.shape[1]))

    for index in range(2, len(plan)):
        received(index)
    halo_first = lax.broadcasted_iota(jnp.int32, (total_rows, LANES), 1) < HALO
    body_rows = pl.ds(PAD, total_rows)
    outer = pl.ds(breadth, LANES)
    fr, fl = from_right[...], from_left[...]
    pbuf[body_rows, outer] = jnp.where(halo_first, fr, fl)
    lbuf[body_rows, outer] = pltpu.roll(jnp.where(halo_first, fl, fr), HALO, 1)
    fine_mask = lane_mask(width, breadth)

    def prepare(chunk, carry):
        start = pl.multiple_of(chunk * CHUNK, CHUNK)
        x = pbuf[pl.ds(start, CHUNK + 2 * PAD), :]
        s = 4.0 * x - near(x)
        q = 4.0 * s - near(s)
        inside = slice(PAD, PAD + CHUNK)
        rows = pl.ds(pl.multiple_of(start + PAD, 8), CHUNK)
        scale = jnp.where(
            start < HALO, up_f, jnp.where(start >= HALO + height, down_f, 1.0)
        )
        mask = fine_mask * scale
        abuf[rows, :] = (lbuf[rows, :] - MASS * x[inside] - q[inside]) * mask
        bbuf[rows, :] = s[inside] * mask
        return carry

    lax.fori_loop(0, total_rows // CHUNK, prepare, 0)

    pltpu.make_async_copy(sums, sums, red_sem.at[1]).wait()
    energy = jnp.sum(jnp.sum(sums[...], axis=0) + part[...])
    cells = float(height * nx * breadth * ny)
    tension = TENSION_BASE + TENSION_GAIN * energy * (1.0 / cells)

    alpha0, beta0, w0 = constants(0, tension)

    def leave(chunk, carry):
        start = pl.multiple_of(chunk * CHUNK, CHUNK)
        rows = pl.ds(start, CHUNK + 2 * PAD)
        g = abuf[rows, :] - tension * bbuf[rows, :]
        r = (g - w0 * operate(g, alpha0, beta0))[PAD : PAD + CHUNK]
        for t in range(tiles + 1):
            at = pl.multiple_of(t * total_rows + start, 8)
            rtile[pl.ds(at, CHUNK), :] = r[:, t * LANES : (t + 1) * LANES]
        return carry

    lax.fori_loop(0, total_rows // CHUNK, leave, 0)

    def paired(ref, rows, count):
        return [
            ref[pl.ds(t * rows, rows // 2, stride=2), :]
            + ref[pl.ds(t * rows + 1, rows // 2, stride=2), :]
            for t in range(count)
        ]

    def restrict(ref, rows, count, halo_matrix):
        xs = paired(ref, rows, count)
        outs = [
            dot2(jnp.concatenate(xs[t : t + 2], axis=1), c2[...])
            for t in range(0, count - 1, 2)
        ]
        outs.append(dot2(xs[-1], halo_matrix[...]))
        return jnp.concatenate(outs, axis=1)

    def spread(ref, columns, rows):
        for t, x in enumerate(columns):
            ref[pl.ds(t * rows, rows // 2, stride=2), :] = x
            ref[pl.ds(t * rows + 1, rows // 2, stride=2), :] = x

    def prolong(ref, e, rows, halo_matrix):
        count = e.shape[1] // LANES
        columns = []
        for t in range(count - 1):
            pair = dot2(e[:, t * LANES : (t + 1) * LANES], p2[...])
            columns += [pair[:, :LANES], pair[:, LANES:]]
        columns.append(dot2(e[:, (count - 1) * LANES :], halo_matrix[...]))
        spread(ref, columns, rows)

    def gathered(ref, rows, count, first_row, n):
        return jnp.concatenate(
            [ref[pl.ds(t * rows + first_row, n), :] for t in range(count)], axis=1
        )

    def store_tiles(ref, value, rows):
        for t in range(value.shape[1] // LANES):
            ref[pl.ds(t * rows, rows), :] = value[:, t * LANES : (t + 1) * LANES]

    rows1, rows2, rows3 = total_rows // 2, total_rows // 4, total_rows // 8
    count1, count2 = tiles // 2 + 1, tiles // 4 + 1

    g1 = restrict(rtile, total_rows, tiles + 1, ch0) * mask1[...]
    alpha1, beta1, w1 = constants(1, tension)
    store_tiles(r1t, g1 - w1 * operate(g1, alpha1, beta1), rows1)
    g2 = restrict(r1t, rows1, count1, ch1) * mask2[...]
    alpha2, beta2, w2 = constants(2, tension)
    store_tiles(r2t, g2 - w2 * operate(g2, alpha2, beta2), rows2)
    pair = paired(r2t, rows2, count2)
    g3 = dot2(jnp.concatenate(pair, axis=1), c3[...]) * mask3[...]

    alpha3, beta3, w3 = constants(3, tension)
    u3 = w3 * g3
    for _ in range(COARSE - 1):
        u3 = (u3 + w3 * (g3 - operate(u3, alpha3, beta3))) * mask3[...]

    wide_pair = dot2(u3, p3[...])
    spread(e2t, [wide_pair[:, :LANES], wide_pair[:, LANES:]], rows2)
    u2 = w2 * g2 + gathered(e2t, rows2, count2, 0, rows2)
    u2 = (u2 + w2 * (g2 - operate(u2, alpha2, beta2))) * mask2[...]
    prolong(e1t, u2, rows1, ph1)
    u1 = w1 * g1 + gathered(e1t, rows1, count1, 0, rows1)
    u1 = (u1 + w1 * (g1 - operate(u1, alpha1, beta1))) * mask1[...]
    prolong(etile0, u1, total_rows, ph0)

    def finish(chunk, carry):
        start = pl.multiple_of(chunk * CHUNK, CHUNK)
        rows = pl.ds(pl.multiple_of(start + HALO, 8), CHUNK + 2 * PAD)
        g = abuf[rows, :] - tension * bbuf[rows, :]
        e = jnp.concatenate(
            [
                etile0[pl.ds(pl.multiple_of(t * total_rows + start + HALO - PAD, 8), CHUNK + 2 * PAD), :]
                for t in range(tiles + 1)
            ],
            axis=1,
        )
        u = w0 * g + e
        u = (u + w0 * (g - operate(u, alpha0, beta0)))[PAD : PAD + CHUNK, :breadth]
        here = pl.ds(pl.multiple_of(start + HALO + PAD, 8), CHUNK)
        out_ref[pl.ds(start, CHUNK), :] = pbuf[here, wide] + u
        return carry

    lax.fori_loop(0, height // CHUNK, finish, 0)

    pltpu.make_async_copy(sums, sums, red_sem.at[0]).wait()
    for index in range(len(plan)):
        @pl.when(plan[index][4])
        def _(index=index):
            copy_of(index).wait_send()


def body(displacement, velocity, load):
    nx, ny = lax.axis_size("gx"), lax.axis_size("gy")
    height, breadth = displacement.shape
    rows, tiles = height + 2 * HALO, breadth // LANES
    padded = (rows + 2 * PAD, breadth + LANES)
    f32, bf16 = jnp.float32, jnp.bfloat16
    widths = [(breadth >> level) + LANES for level in range(3)] + [LANES]

    def vmem(*shape, dtype=f32):
        return pltpu.VMEM(shape, dtype)

    def tiled(level):
        return vmem(widths[level] // LANES * (rows >> level), LANES)

    scratch = [
        vmem(height, breadth), vmem(height, breadth),
        vmem(*padded), vmem(*padded),
        vmem(height, LANES), vmem(height, LANES),
        vmem(rows, LANES), vmem(rows, LANES),
        vmem(8, breadth), vmem(8, height), vmem(8, height), vmem(*padded), vmem(*padded),
        tiled(0), tiled(0), tiled(1), tiled(1), tiled(2), tiled(2),
        vmem(rows // 2, widths[1]), vmem(rows // 4, widths[2]), vmem(rows // 8, widths[3]),
        vmem(2 * LANES, LANES, dtype=bf16), vmem(LANES, LANES, dtype=bf16),
        vmem(LANES, LANES, dtype=bf16), vmem(2 * LANES, LANES, dtype=bf16),
        vmem(LANES, 2 * LANES, dtype=bf16), vmem(LANES, LANES, dtype=bf16),
        vmem(LANES, LANES, dtype=bf16), vmem(LANES, 2 * LANES, dtype=bf16),
        vmem(1, LANES),
        vmem(nx * ny - 1, 1, LANES),
        pltpu.SemaphoreType.DMA((3,)),
        pltpu.SemaphoreType.DMA((12,)),
        pltpu.SemaphoreType.DMA((12,)),
        pltpu.SemaphoreType.DMA((2,)),
    ]

    def kernel(*refs):
        kernel_body(nx, ny, height, breadth, *refs)

    return pl.pallas_call(
        kernel,
        out_shape=jax.ShapeDtypeStruct((height, breadth), f32),
        in_specs=[pl.BlockSpec(memory_space=pltpu.HBM)] * 3,
        out_specs=pl.BlockSpec(memory_space=pltpu.VMEM),
        scratch_shapes=scratch,
        compiler_params=pltpu.CompilerParams(
            collective_id=0, has_side_effects=True, vmem_limit_bytes=62 * 1024 * 1024
        ),
    )(displacement, velocity, load)


def solution(mesh):
    placed = (P("gx", "gy"), P("gx", "gy"), P("gx", "gy"))
    return jax.shard_map(body, mesh=mesh, in_specs=placed, out_specs=P("gx", "gy"), check_vma=False)
```

```python
import jax
import jax.numpy as jnp
from jax import lax
from jax.experimental import pallas as pl
from jax.experimental.pallas import tpu as pltpu
from jax.sharding import PartitionSpec as P

COARSE = 3
MASS = 0.0001
DAMPING = 0.5
TENSION_BASE = 1.0
TENSION_GAIN = 3.0

HALO = 64
PAD = 8
LANES = 128
CHUNK = 64
DOWN = 256
UP = 128
MESH = pl.DeviceIdType.MESH


def near(x):
    rows, cols = x.shape
    across = pltpu.roll(x, 1, 1) + pltpu.roll(x, cols - 1, 1)
    return across + (pltpu.roll(x, 1, 0) + pltpu.roll(x, rows - 1, 0))


def constants(level, tension):
    alpha = 1.0 / 16.0**level
    beta = tension * (1.0 / 4.0**level)
    weight = DAMPING / (MASS + 20.0 * alpha + 4.0 * beta)
    return alpha, beta, weight


def operate(x, alpha, beta):
    y = (4.0 * alpha + beta) * x - alpha * near(x)
    return MASS * x + (4.0 * y - near(y))


def dot2(x, matrix):
    high = x.astype(jnp.bfloat16)
    low = (x - high.astype(jnp.float32)).astype(jnp.bfloat16)
    return jnp.dot(high, matrix, preferred_element_type=jnp.float32) + jnp.dot(
        low, matrix, preferred_element_type=jnp.float32
    )


def halo_parent(lane, width):
    right = lane < width
    left = lane >= LANES - width
    upper = LANES - width // 2 + ((lane - (LANES - width)) >> 1)
    return jnp.where(right, lane >> 1, jnp.where(left, upper, -1))


def last_parent(lane, centre, width):
    halo = lane - centre
    right = centre // 2 + (halo >> 1)
    left = LANES - width // 2 + ((halo - (LANES - width)) >> 1)
    outer = jnp.where(halo < width, right, jnp.where(halo >= LANES - width, left, -1))
    return jnp.where(lane < centre, lane >> 1, outer)


def build(ref, parent, value, transposed):
    fine_dim = 1 if transposed else 0
    fine = lax.broadcasted_iota(jnp.int32, ref.shape, fine_dim)
    coarse = lax.broadcasted_iota(jnp.int32, ref.shape, 1 - fine_dim)
    ref[...] = jnp.where(parent(fine) == coarse, value, 0.0).astype(jnp.bfloat16)


def kernel_body(
    nx, ny, height, breadth,
    d_hbm, v_hbm, load_hbm, out_ref,
    dbuf, vbuf, pbuf, lbuf, lmsg, rmsg, from_right, from_left, edge, rim, rim_in, abuf, bbuf,
    rtile, etile0, r1t, e1t, r2t, e2t,
    mask1, mask2, mask3,
    c2, ch0, ch1, c3, p2, ph0, ph1, p3,
    part, sums,
    in_sem, send_sem, recv_sem, red_sem,
):
    gx = lax.axis_index("gx")
    gy = lax.axis_index("gy")
    has_up = gx > 0
    has_down = gx < nx - 1
    has_left = gy > 0
    has_right = gy < ny - 1
    total_rows = height + 2 * HALO
    tiles = breadth // LANES
    width = breadth + LANES

    barrier = pltpu.get_barrier_semaphore()
    def every_other(action):
        for dx in range(nx):
            ahead = gx + dx
            tx = jnp.where(ahead >= nx, ahead - nx, ahead)

            def at(dy, carry, dx=dx, tx=tx):
                along = gy + dy
                action(dx * ny + dy - 1, (tx, jnp.where(along >= ny, along - ny, along)))
                return carry

            lax.fori_loop(1 if dx == 0 else 0, ny, at, 0, unroll=ny <= 8)

    def greet(slot, device):
        pl.semaphore_signal(barrier, 1, device_id=device, device_id_type=MESH)

    every_other(greet)

    centre_rows = pl.ds(PAD + HALO, height)
    loads = [
        pltpu.make_async_copy(d_hbm, dbuf, in_sem.at[0]),
        pltpu.make_async_copy(v_hbm, vbuf, in_sem.at[1]),
        pltpu.make_async_copy(load_hbm, lbuf.at[centre_rows, pl.ds(0, breadth)], in_sem.at[2]),
    ]
    for copy in loads:
        copy.start()

    zero_rows = jnp.zeros((PAD, width), jnp.float32)
    for buf in (pbuf, lbuf, abuf, bbuf):
        buf[pl.ds(0, PAD), :] = zero_rows
        buf[pl.ds(PAD + total_rows, PAD), :] = zero_rows

    def clear(ref, start, rows, cols):
        ref[pl.ds(start, rows), pl.ds(0, cols)] = jnp.zeros((rows, cols), jnp.float32)

    @pl.when(jnp.logical_not(has_up))
    def _():
        for buf in (pbuf, lbuf):
            clear(buf, PAD, HALO, breadth)
        clear(from_right, 0, HALO, LANES)
        clear(from_left, 0, HALO, LANES)

    @pl.when(jnp.logical_not(has_down))
    def _():
        for buf in (pbuf, lbuf):
            clear(buf, PAD + HALO + height, HALO, breadth)
        clear(from_right, HALO + height, HALO, LANES)
        clear(from_left, HALO + height, HALO, LANES)
        clear(edge, 0, 8, breadth)

    @pl.when(jnp.logical_not(has_right))
    def _():
        clear(from_right, 0, total_rows, LANES)
        clear(rim_in, 0, 8, height)

    @pl.when(jnp.logical_not(has_left))
    def _():
        clear(from_left, 0, total_rows, LANES)

    loads[0].wait()
    loads[1].wait()
    pbuf[centre_rows, pl.ds(0, breadth)] = dbuf[...] + vbuf[...]
    rim[...] = jnp.transpose(pbuf[centre_rows, pl.ds(0, LANES)])[:8]
    loads[2].wait()

    lane = lax.broadcasted_iota(jnp.int32, (height, LANES), 1)
    first = lane < HALO
    lmsg[...] = jnp.where(
        first,
        pbuf[centre_rows, pl.ds(0, LANES)],
        pltpu.roll(lbuf[centre_rows, pl.ds(0, LANES)], HALO, 1),
    )
    end = pl.ds(breadth - LANES, LANES)
    rmsg[...] = jnp.where(
        first, pltpu.roll(lbuf[centre_rows, end], HALO, 1), pbuf[centre_rows, end]
    )

    wide = pl.ds(0, breadth)
    top_src = pl.ds(PAD + HALO, HALO)
    bottom_src = pl.ds(PAD + height, HALO)
    top_dst = pl.ds(PAD, HALO)
    bottom_dst = pl.ds(PAD + HALO + height, HALO)
    mid = pl.ds(HALO, height)
    upper, lower = pl.ds(0, HALO), pl.ds(height - HALO, HALO)
    dst_top, dst_bottom = pl.ds(0, HALO), pl.ds(HALO + height, HALO)
    both = jnp.logical_and
    plan = [
        (pbuf.at[pl.ds(PAD + HALO, 8), wide], edge, -1, 0, has_up, has_down),
        (rim, rim_in, 0, -1, has_left, has_right),
        (pbuf.at[top_src, wide], pbuf.at[bottom_dst, wide], -1, 0, has_up, has_down),
        (pbuf.at[bottom_src, wide], pbuf.at[top_dst, wide], 1, 0, has_down, has_up),
        (lmsg, from_right.at[mid], 0, -1, has_left, has_right),
        (rmsg, from_left.at[mid], 0, 1, has_right, has_left),
        (lmsg.at[upper], from_right.at[dst_bottom], -1, -1, both(has_up, has_left), both(has_down, has_right)),
        (lmsg.at[lower], from_right.at[dst_top], 1, -1, both(has_down, has_left), both(has_up, has_right)),
        (rmsg.at[upper], from_left.at[dst_bottom], -1, 1, both(has_up, has_right), both(has_down, has_left)),
        (rmsg.at[lower], from_left.at[dst_top], 1, 1, both(has_down, has_right), both(has_up, has_left)),
        (lbuf.at[top_src, wide], lbuf.at[bottom_dst, wide], -1, 0, has_up, has_down),
        (lbuf.at[bottom_src, wide], lbuf.at[top_dst, wide], 1, 0, has_down, has_up),
    ]

    def copy_of(index):
        source, target, dx, dy, _, _ = plan[index]
        return pltpu.make_async_remote_copy(
            src_ref=source,
            dst_ref=target,
            send_sem=send_sem.at[index],
            recv_sem=recv_sem.at[index],
            device_id=(gx + dx, gy + dy),
            device_id_type=MESH,
        )

    def received(index):
        @pl.when(plan[index][5])
        def _():
            copy_of(index).wait_recv()

    pl.semaphore_wait(barrier, nx * ny - 1)
    for index in range(len(plan)):
        @pl.when(plan[index][4])
        def _(index=index):
            copy_of(index).start()

    x = pbuf[centre_rows, wide]
    row = lax.broadcasted_iota(jnp.int32, (height, breadth), 0)
    col = lax.broadcasted_iota(jnp.int32, (height, breadth), 1)
    down = jnp.where(row < height - 1, pltpu.roll(x, height - 1, 0) - x, 0.0)
    right = jnp.where(col < breadth - 1, pltpu.roll(x, breadth - 1, 1) - x, 0.0)
    inner = jnp.sum(down * down + right * right, axis=0, keepdims=True)
    inner = sum(inner[:, t * LANES : (t + 1) * LANES] for t in range(tiles))

    last_column = jnp.transpose(x[:, breadth - LANES :])[LANES - 1 :]

    received(0)
    received(1)
    below = edge[pl.ds(0, 1), :] - x[height - 1 : height, :]
    below = below * below
    below = sum(below[:, t * LANES : (t + 1) * LANES] for t in range(tiles))
    beside = rim_in[pl.ds(0, 1), :] - last_column
    beside = beside * beside
    beside = sum(beside[:, t * LANES : (t + 1) * LANES] for t in range(height // LANES))
    part[...] = inner + below + beside

    def give(slot, device):
        pltpu.make_async_remote_copy(
            src_ref=part,
            dst_ref=sums.at[slot],
            send_sem=red_sem.at[0],
            recv_sem=red_sem.at[1],
            device_id=device,
            device_id_type=MESH,
        ).start()

    every_other(give)

    build(c2, lambda i: i >> 1, 0.25, False)
    build(p2, lambda i: i >> 1, 1.0, True)
    build(ch0, lambda i: halo_parent(i, HALO), 0.25, False)
    build(ph0, lambda i: halo_parent(i, HALO), 1.0, True)
    build(ch1, lambda i: halo_parent(i, HALO // 2), 0.25, False)
    build(ph1, lambda i: halo_parent(i, HALO // 2), 1.0, True)
    build(c3, lambda i: last_parent(i, LANES, HALO // 4), 0.25, False)
    build(p3, lambda i: last_parent(i, LANES, HALO // 4), 1.0, True)
    up_f, down_f = has_up.astype(jnp.float32), has_down.astype(jnp.float32)
    left_f, right_f = has_left.astype(jnp.float32), has_right.astype(jnp.float32)

    def lane_mask(cols, centre):
        i = lax.broadcasted_iota(jnp.int32, (1, cols), 1)
        outside = jnp.where(i - centre < (cols - centre) // 2, right_f, left_f)
        return jnp.where(i < centre, 1.0, outside)

    for level, mask in ((1, mask1), (2, mask2), (3, mask3)):
        rim, core = HALO >> level, height >> level
        cols = lane_mask(mask.shape[1], breadth >> level)
        mask[pl.ds(0, rim), :] = jnp.broadcast_to(cols * up_f, (rim, mask.shape[1]))
        mask[pl.ds(rim, core), :] = jnp.broadcast_to(cols, (core, mask.shape[1]))
        mask[pl.ds(rim + core, rim), :] = jnp.broadcast_to(cols * down_f, (rim, mask.shape[1]))

    for index in range(2, len(plan)):
        received(index)
    halo_first = lax.broadcasted_iota(jnp.int32, (total_rows, LANES), 1) < HALO
    body_rows = pl.ds(PAD, total_rows)
    outer = pl.ds(breadth, LANES)
    fr, fl = from_right[...], from_left[...]
    pbuf[body_rows, outer] = jnp.where(halo_first, fr, fl)
    lbuf[body_rows, outer] = pltpu.roll(jnp.where(halo_first, fl, fr), HALO, 1)
    fine_mask = lane_mask(width, breadth)

    def prepare(chunk, carry):
        start = pl.multiple_of(chunk * CHUNK, CHUNK)
        x = pbuf[pl.ds(start, CHUNK + 2 * PAD), :]
        s = 4.0 * x - near(x)
        q = 4.0 * s - near(s)
        inside = slice(PAD, PAD + CHUNK)
        rows = pl.ds(pl.multiple_of(start + PAD, 8), CHUNK)
        scale = jnp.where(
            start < HALO, up_f, jnp.where(start >= HALO + height, down_f, 1.0)
        )
        mask = fine_mask * scale
        abuf[rows, :] = (lbuf[rows, :] - MASS * x[inside] - q[inside]) * mask
        bbuf[rows, :] = s[inside] * mask
        return carry

    lax.fori_loop(0, total_rows // CHUNK, prepare, 0, unroll=True)

    pltpu.make_async_copy(sums, sums, red_sem.at[1]).wait()
    energy = jnp.sum(jnp.sum(sums[...], axis=0) + part[...])
    cells = float(height * nx * breadth * ny)
    tension = TENSION_BASE + TENSION_GAIN * energy * (1.0 / cells)

    alpha0, beta0, w0 = constants(0, tension)

    def leave(chunk, carry):
        start = pl.multiple_of(chunk * DOWN, DOWN)
        rows = pl.ds(start, DOWN + 2 * PAD)
        g = abuf[rows, :] - tension * bbuf[rows, :]
        r = (g - w0 * operate(g, alpha0, beta0))[PAD : PAD + DOWN]
        for t in range(tiles + 1):
            at = pl.multiple_of(t * total_rows + start, 8)
            rtile[pl.ds(at, DOWN), :] = r[:, t * LANES : (t + 1) * LANES]
        return carry

    lax.fori_loop(0, total_rows // DOWN, leave, 0)

    def paired(ref, rows, count):
        return [
            ref[pl.ds(t * rows, rows // 2, stride=2), :]
            + ref[pl.ds(t * rows + 1, rows // 2, stride=2), :]
            for t in range(count)
        ]

    def restrict(ref, rows, count, halo_matrix):
        xs = paired(ref, rows, count)
        outs = [
            dot2(jnp.concatenate(xs[t : t + 2], axis=1), c2[...])
            for t in range(0, count - 1, 2)
        ]
        outs.append(dot2(xs[-1], halo_matrix[...]))
        return jnp.concatenate(outs, axis=1)

    def spread(ref, columns, rows):
        for t, x in enumerate(columns):
            ref[pl.ds(t * rows, rows // 2, stride=2), :] = x
            ref[pl.ds(t * rows + 1, rows // 2, stride=2), :] = x

    def prolong(ref, e, rows, halo_matrix):
        count = e.shape[1] // LANES
        columns = []
        for t in range(count - 1):
            pair = dot2(e[:, t * LANES : (t + 1) * LANES], p2[...])
            columns += [pair[:, :LANES], pair[:, LANES:]]
        columns.append(dot2(e[:, (count - 1) * LANES :], halo_matrix[...]))
        spread(ref, columns, rows)

    def gathered(ref, rows, count, first_row, n):
        return jnp.concatenate(
            [ref[pl.ds(t * rows + first_row, n), :] for t in range(count)], axis=1
        )

    def store_tiles(ref, value, rows):
        for t in range(value.shape[1] // LANES):
            ref[pl.ds(t * rows, rows), :] = value[:, t * LANES : (t + 1) * LANES]

    rows1, rows2, rows3 = total_rows // 2, total_rows // 4, total_rows // 8
    count1, count2 = tiles // 2 + 1, tiles // 4 + 1

    g1 = restrict(rtile, total_rows, tiles + 1, ch0) * mask1[...]
    alpha1, beta1, w1 = constants(1, tension)
    store_tiles(r1t, g1 - w1 * operate(g1, alpha1, beta1), rows1)
    g2 = restrict(r1t, rows1, count1, ch1) * mask2[...]
    alpha2, beta2, w2 = constants(2, tension)
    store_tiles(r2t, g2 - w2 * operate(g2, alpha2, beta2), rows2)
    pair = paired(r2t, rows2, count2)
    g3 = dot2(jnp.concatenate(pair, axis=1), c3[...]) * mask3[...]

    alpha3, beta3, w3 = constants(3, tension)
    u3 = w3 * g3
    for _ in range(COARSE - 1):
        u3 = (u3 + w3 * (g3 - operate(u3, alpha3, beta3))) * mask3[...]

    wide_pair = dot2(u3, p3[...])
    spread(e2t, [wide_pair[:, :LANES], wide_pair[:, LANES:]], rows2)
    u2 = w2 * g2 + gathered(e2t, rows2, count2, 0, rows2)
    u2 = (u2 + w2 * (g2 - operate(u2, alpha2, beta2))) * mask2[...]
    prolong(e1t, u2, rows1, ph1)
    u1 = w1 * g1 + gathered(e1t, rows1, count1, 0, rows1)
    u1 = (u1 + w1 * (g1 - operate(u1, alpha1, beta1))) * mask1[...]
    prolong(etile0, u1, total_rows, ph0)

    def finish(chunk, carry):
        start = pl.multiple_of(chunk * UP, UP)
        rows = pl.ds(pl.multiple_of(start + HALO, 8), UP + 2 * PAD)
        g = abuf[rows, :] - tension * bbuf[rows, :]
        e = jnp.concatenate(
            [
                etile0[pl.ds(pl.multiple_of(t * total_rows + start + HALO - PAD, 8), UP + 2 * PAD), :]
                for t in range(tiles + 1)
            ],
            axis=1,
        )
        u = w0 * g + e
        u = (u + w0 * (g - operate(u, alpha0, beta0)))[PAD : PAD + UP, :breadth]
        here = pl.ds(pl.multiple_of(start + HALO + PAD, 8), UP)
        out_ref[pl.ds(start, UP), :] = pbuf[here, wide] + u
        return carry

    lax.fori_loop(0, height // UP, finish, 0)

    pltpu.make_async_copy(sums, sums, red_sem.at[0]).wait()
    for index in range(len(plan)):
        @pl.when(plan[index][4])
        def _(index=index):
            copy_of(index).wait_send()


def body(displacement, velocity, load):
    nx, ny = lax.axis_size("gx"), lax.axis_size("gy")
    height, breadth = displacement.shape
    rows, tiles = height + 2 * HALO, breadth // LANES
    padded = (rows + 2 * PAD, breadth + LANES)
    f32, bf16 = jnp.float32, jnp.bfloat16
    widths = [(breadth >> level) + LANES for level in range(3)] + [LANES]

    def vmem(*shape, dtype=f32):
        return pltpu.VMEM(shape, dtype)

    def tiled(level):
        return vmem(widths[level] // LANES * (rows >> level), LANES)

    scratch = [
        vmem(height, breadth), vmem(height, breadth),
        vmem(*padded), vmem(*padded),
        vmem(height, LANES), vmem(height, LANES),
        vmem(rows, LANES), vmem(rows, LANES),
        vmem(8, breadth), vmem(8, height), vmem(8, height), vmem(*padded), vmem(*padded),
        tiled(0), tiled(0), tiled(1), tiled(1), tiled(2), tiled(2),
        vmem(rows // 2, widths[1]), vmem(rows // 4, widths[2]), vmem(rows // 8, widths[3]),
        vmem(2 * LANES, LANES, dtype=bf16), vmem(LANES, LANES, dtype=bf16),
        vmem(LANES, LANES, dtype=bf16), vmem(2 * LANES, LANES, dtype=bf16),
        vmem(LANES, 2 * LANES, dtype=bf16), vmem(LANES, LANES, dtype=bf16),
        vmem(LANES, LANES, dtype=bf16), vmem(LANES, 2 * LANES, dtype=bf16),
        vmem(1, LANES),
        vmem(nx * ny - 1, 1, LANES),
        pltpu.SemaphoreType.DMA((3,)),
        pltpu.SemaphoreType.DMA((12,)),
        pltpu.SemaphoreType.DMA((12,)),
        pltpu.SemaphoreType.DMA((2,)),
    ]

    def kernel(*refs):
        kernel_body(nx, ny, height, breadth, *refs)

    return pl.pallas_call(
        kernel,
        out_shape=jax.ShapeDtypeStruct((height, breadth), f32),
        in_specs=[pl.BlockSpec(memory_space=pltpu.HBM)] * 3,
        out_specs=pl.BlockSpec(memory_space=pltpu.VMEM),
        scratch_shapes=scratch,
        compiler_params=pltpu.CompilerParams(
            collective_id=0, has_side_effects=True, vmem_limit_bytes=62 * 1024 * 1024
        ),
    )(displacement, velocity, load)


def solution(mesh):
    placed = (P("gx", "gy"), P("gx", "gy"), P("gx", "gy"))
    return jax.shard_map(body, mesh=mesh, in_specs=placed, out_specs=P("gx", "gy"), check_vma=False)
```
